32 devices in a mesh: bin: 4 (over y, core), fsdp: 8 (over z, x).
Axes of the slice: x: 2, y: 2, z: 4, core: 2. Of those that a mesh axis runs over, the one named last changes fastest.
Arguments:
- tokens: bfloat16 [64, 256, 1152], P(('bin', 'fsdp')), may hold values from -6 to 6
- features: bfloat16 [64, 256, 768], P(('bin', 'fsdp')), may hold values from -6 to 6
- cotangent: bfloat16 [64, 256, 1152], P(('bin', 'fsdp')), may hold values from -6 to 6
- bin_counts: int32 [4], replicated, may hold values from 1 to 10, 32 in all
- timesteps: int32 [4], replicated, may hold values from 0 to 999
- labels: int32 [4], replicated, may hold values from 0 to 999
- qkv_weight: bfloat16 [1152, 3456], P('fsdp'), may hold values from -0.25 to 0.25
- attn_weight: bfloat16 [1152, 1152], P('fsdp'), may hold values from -0.75 to 0.75
- up_weight: bfloat16 [1152, 4608], P('fsdp'), may hold values from -0.1875 to 0.1875
- down_weight: bfloat16 [4608, 1152], P('fsdp'), may hold values from -0.09375 to 0.09375
- repa_first: bfloat16 [1152, 2048], P('fsdp'), may hold values from -0.1875 to 0.1875
- repa_second: bfloat16 [2048, 2048], P('fsdp'), may hold values from -0.125 to 0.125
- repa_third: bfloat16 [2048, 768], P('fsdp'), may hold values from -0.125 to 0.125
- ada_weight: bfloat16 [1152, 6912], P(None, 'fsdp'), may hold values from -0.1875 to 0.1875
- ada_bias: bfloat16 [6912], P('fsdp'), may hold values from -3 to 3
- time_first: bfloat16 [256, 1152], P('fsdp'), may hold values from -0.5 to 0.5
- time_second: bfloat16 [1152, 1152], P('fsdp'), may hold values from -0.1875 to 0.1875
- label_table: bfloat16 [1000, 1152], P(None, 'fsdp'), may hold values from -6 to 6
Outputs:
- out: bfloat16 [64, 256, 1152], P(('bin', 'fsdp'))
- grad_input: float32 [64, 256, 1152], P(('bin', 'fsdp'))
- grad_qkv: float32 [1152, 3456], P('fsdp')
- grad_attn: float32 [1152, 1152], P('fsdp')
- grad_up: float32 [1152, 4608], P('fsdp')
- grad_down: float32 [4608, 1152], P('fsdp')
- grad_first: float32 [1152, 2048], P('fsdp')
- grad_second: float32 [2048, 2048], P('fsdp')
- grad_third: float32 [2048, 768], P('fsdp')
- grad_ada: float32 [1152, 6912], P(None, 'fsdp')
- grad_bias: float32 [6912], P('fsdp')
- grad_time_first: float32 [256, 1152], P('fsdp')
- grad_time_second: float32 [1152, 1152], P('fsdp')
- grad_table: float32 [1000, 1152], P(None, 'fsdp')
The draws below stay inside these ranges and needn't reach their ends.
Inputs may be any that keep to these rules, and one draw needn't show every extreme that they name: `bin_counts`: the counts of all bins sum to 32.
All inputs are finite; a program needn't handle non-finite values.
Results may differ from the reference program's by a relative error of at most 0.025.
Values may be sent and summed in bfloat16 or wider, within the bound.
No kernel may reach another device: no remote copies, remote signals or barrier semaphores. Data moves between devices by JAX's collectives and lax.ppermute only.
A program may use at most 192 MiB of HBM per device.

```python
import math
import jax
import jax.numpy as jnp
import numpy as np
from jax import lax

D = 1152
HEADS = 16
FF = 4608
PROJ = 2048
ZDIM = 768
CLASSES = 1000
FREQ = 256
STEPS = 1000
PATCHES = 256
BINS = 4
BIN_CAP = 16
IMAGES = 64


def touch_ends(values, key, smallest, top_value):
    place = [jax.random.randint(jax.random.fold_in(key, axis), (), 0, length) for axis, length in enumerate(values.shape)]
    widest = values.shape.index(max(values.shape))
    next_to = place[:widest] + [(place[widest] + 1) % values.shape[widest]] + place[widest + 1:]
    return values.at[tuple(place)].set(smallest).at[tuple(next_to)].set(top_value)


def steps_of(key, shape, cuts, low, high):
    loudness, own = 1.0, jax.random.fold_in(key, 6)
    for position, blocks in cuts:
        steps = jnp.exp(jax.random.uniform(jax.random.fold_in(own, position), (blocks,), jnp.float32, low / len(cuts), high / len(cuts)))
        loudness = loudness * jnp.repeat(steps, shape[position] // blocks).reshape([-1 if axis == position else 1 for axis in range(len(shape))])
    return loudness


def length_profile(number_of, total, most, slope):
    loads = [(1 << 20) // math.isqrt(grade ** slope) + 1 for grade in range(2, number_of + 1)]
    rest, given = total - most - (number_of - 1), [1] * (number_of - 1)
    while rest > 0:
        movable = [i for i in range(number_of - 1) if given[i] < most]
        mass, left = sum([loads[i] for i in movable]), rest
        for i in movable:
            extra = min(most - given[i], max(1, left * loads[i] // mass), rest)
            given[i] = given[i] + extra
            rest = rest - extra
    return np.array([most] + given)


def ragged_sizes(own_key, count, total, reach, slope):
    if count == 2:
        one = jax.random.randint(own_key, (), max(1, total - reach), min(reach, total - 1) + 1)
        return jnp.stack([one, total - one])
    lengths = jnp.asarray(length_profile(count, total, reach, slope), jnp.int32)
    pairs = (count - 1) // 2
    donor, taker = lengths[1:1 + 2 * pairs:2], lengths[2:2 + 2 * pairs:2]
    room = jnp.minimum(donor - 1, reach - taker)
    moved = jax.random.randint(jax.random.fold_in(own_key, 1), (pairs,), 0, 1 << 20) % (room + 1)
    lengths = lengths.at[1:1 + 2 * pairs:2].set(donor - moved).at[2:2 + 2 * pairs:2].set(taker + moved)
    return lengths[jax.random.permutation(jax.random.fold_in(own_key, 2), count)]


def scatter_about(key, shape, width, reach, cuts=(), kind=jnp.bfloat16):
    array = width * jax.random.normal(key, shape, jnp.float32)
    if cuts:
        array = array * steps_of(key, shape, cuts, -0.22, 0.18)
    return jnp.clip(array, -reach, reach).astype(kind)


def setup_inputs(seed: int = 0) -> dict:
    key_of = jax.random.split(jax.random.key(seed), 19)
    tokens = scatter_about(key_of[0], (IMAGES, PATCHES, D), 1.0, 6.0, ((0, 32),))
    features = scatter_about(key_of[1], (IMAGES, PATCHES, ZDIM), 1.0, 6.0, ((0, 32),))
    cotangent = scatter_about(key_of[2], (IMAGES, PATCHES, D), 1.0, 6.0, ((0, 32),))
    bin_counts = ragged_sizes(key_of[3], BINS, BINS * BIN_CAP // 2, 5 * BIN_CAP // 8, 1).astype(jnp.int32)
    timesteps = touch_ends(jax.random.randint(key_of[4], (BINS,), 0, STEPS), jax.random.fold_in(key_of[4], 1), 0, STEPS - 1).astype(jnp.int32)
    labels = touch_ends(jax.random.randint(key_of[5], (BINS,), 0, CLASSES), jax.random.fold_in(key_of[5], 1), 0, CLASSES - 1).astype(jnp.int32)
    qkv_weight = scatter_about(key_of[6], (D, 3 * D), (D // 2) ** -0.5, 0.25, ((0, 8),))
    attn_weight = scatter_about(key_of[7], (D, D), (D // 16) ** -0.5, 0.75, ((0, 8),))
    up_weight = scatter_about(key_of[8], (D, FF), D ** -0.5, 0.1875, ((0, 8),))
    down_weight = scatter_about(key_of[9], (FF, D), FF ** -0.5, 0.09375, ((0, 8),))
    repa_first = scatter_about(key_of[10], (D, PROJ), D ** -0.5, 0.1875, ((0, 8),))
    repa_second = scatter_about(key_of[11], (PROJ, PROJ), PROJ ** -0.5, 0.125, ((0, 8),))
    repa_third = scatter_about(key_of[12], (PROJ, ZDIM), PROJ ** -0.5, 0.125, ((0, 8),))
    ada_weight = scatter_about(key_of[13], (D, 6 * D), D ** -0.5, 0.1875, ((1, 8),))
    ada_bias = scatter_about(key_of[14], (6 * D,), 0.5, 3.0, ((0, 8),))
    time_first = scatter_about(key_of[15], (FREQ, D), (FREQ // 2) ** -0.5, 0.5, ((0, 8),))
    time_second = scatter_about(key_of[16], (D, D), D ** -0.5, 0.1875, ((0, 8),))
    label_table = scatter_about(key_of[17], (CLASSES, D), 1.0, 6.0, ((1, 8),))
    return dict(tokens=tokens, features=features, cotangent=cotangent, bin_counts=bin_counts, timesteps=timesteps, labels=labels, qkv_weight=qkv_weight, attn_weight=attn_weight, up_weight=up_weight, down_weight=down_weight, repa_first=repa_first, repa_second=repa_second, repa_third=repa_third, ada_weight=ada_weight, ada_bias=ada_bias, time_first=time_first, time_second=time_second, label_table=label_table)


@jax.custom_vjp
def low(v):
    return lax.optimization_barrier(v.astype(jnp.bfloat16)).astype(jnp.float32)

@jax.custom_vjp
def low_back(v):
    return v

def low_keep(v):
    return (low(v), None)

def low_pass(kept, grad):
    return (grad,)

def back_keep(v):
    return (v, None)

def back_low(kept, grad):
    return (low(grad),)
low.defvjp(low_keep, low_pass)
low_back.defvjp(back_keep, back_low)
lambda_repa = 0.5
eps_norm = 1e-06

def matmul(first_op, second_op):
    return jnp.matmul(first_op, second_op, precision=lax.Precision.HIGHEST)

def normalize(values):
    row_mean = lax.optimization_barrier(jnp.mean(values, axis=-1, keepdims=True))
    centred = values - row_mean
    return centred * lax.rsqrt(lax.optimization_barrier(jnp.mean(centred * centred, axis=-1, keepdims=True)) + eps_norm)

def condition_of(weights, timesteps, labels):
    stamp_first, stamp_second, ada_w, ada_b, table_w = weights
    half_freq = FREQ // 2
    frequency = jnp.exp(-math.log(10000.0) * jnp.arange(half_freq, dtype=jnp.float32) / half_freq)
    angles = timesteps.astype(jnp.float32)[:, None] * frequency[None, :]
    embedded = jnp.concatenate([jnp.cos(angles), jnp.sin(angles)], axis=-1)
    time_hidden = jax.nn.silu(matmul(embedded, stamp_first))
    condition = matmul(time_hidden, stamp_second) + jnp.take(table_w, labels, axis=0)
    return matmul(jax.nn.silu(condition), ada_w) + ada_b

def block_group(weights, values, modul, targets, validity):
    qkv_w, attn_w, up_w, down_w, first_w, second_w, third_w = weights
    image_count, patches, model_width = values.shape
    head_size = model_width // HEADS
    inv_root = 1.0 / math.sqrt(head_size)
    shift_attn, scale_attn, gate_attn, shift_mlp, scale_mlp, gate_mlp = jnp.split(modul[:, None, :], 6, axis=-1)
    first_in = low(normalize(values) * (1.0 + scale_attn) + shift_attn)
    qkv_act = low(low_back(matmul(first_in, qkv_w))).reshape(image_count, patches, 3, HEADS, head_size)
    query_heads = qkv_act[:, :, 0]
    key_heads = qkv_act[:, :, 1]
    value_heads = qkv_act[:, :, 2]
    scores = jnp.einsum('gqhe,gkhe->ghqk', query_heads, key_heads, precision=lax.Precision.HIGHEST) * inv_root
    scores = low_back(scores)
    row_max = lax.optimization_barrier(jnp.max(scores, axis=-1, keepdims=True))
    exponent = jnp.exp(scores - row_max)
    attn_probs = exponent / lax.optimization_barrier(jnp.sum(exponent, axis=-1, keepdims=True))
    mixed_heads = jnp.einsum('ghqk,gkhe->gqhe', low(attn_probs), value_heads, precision=lax.Precision.HIGHEST)
    mixed_heads = low(low_back(mixed_heads.reshape(image_count, patches, model_width)))
    middle = values + gate_attn * low_back(matmul(mixed_heads, attn_w))
    second_in = low(normalize(middle) * (1.0 + scale_mlp) + shift_mlp)
    up_act = low(jax.nn.gelu(low_back(matmul(second_in, up_w)), approximate=True))
    output = middle + gate_mlp * low_back(matmul(up_act, down_w))
    output_low = low(output)
    first_act = low(jax.nn.silu(low_back(matmul(output_low, first_w))))
    second_act = low(jax.nn.silu(low_back(matmul(first_act, second_w))))
    projected = low_back(matmul(second_act, third_w))
    unit_proj = projected * lax.rsqrt(lax.optimization_barrier(jnp.sum(projected * projected, axis=-1, keepdims=True)) + eps_norm)
    unit_target = targets * lax.rsqrt(lax.optimization_barrier(jnp.sum(targets * targets, axis=-1, keepdims=True)) + eps_norm)
    cosine = lax.optimization_barrier(jnp.sum(unit_proj * unit_target, axis=-1))
    return (output, -lambda_repa * ZDIM * jnp.sum(cosine * validity[:, None]))

def reference(tokens, features, cotangent, bin_counts, timesteps, labels, qkv_weight, attn_weight, up_weight, down_weight, repa_first, repa_second, repa_third, ada_weight, ada_bias, time_first, time_second, label_table):
    slots = jnp.arange(IMAGES) % BIN_CAP
    owners = jnp.arange(IMAGES) // BIN_CAP
    valid_mask = (slots < jnp.take(bin_counts, owners)).astype(jnp.float32)
    params = (qkv_weight.astype(jnp.float32), attn_weight.astype(jnp.float32), up_weight.astype(jnp.float32), down_weight.astype(jnp.float32), repa_first.astype(jnp.float32), repa_second.astype(jnp.float32), repa_third.astype(jnp.float32), ada_weight.astype(jnp.float32), ada_bias.astype(jnp.float32), time_first.astype(jnp.float32), time_second.astype(jnp.float32), label_table.astype(jnp.float32))
    inputs = tokens.astype(jnp.float32)
    targets = features.astype(jnp.float32)
    group_size = 8
    step_count = IMAGES // group_size
    stepper = jax.checkpoint(block_group)

    def forward(weights, values):
        modulation = condition_of((weights[9], weights[10], weights[7], weights[8], weights[11]), timesteps, labels)
        per_image = jnp.repeat(modulation, BIN_CAP, axis=0)
        block_weights = (weights[0], weights[1], weights[2], weights[3], weights[4], weights[5], weights[6])

        def scan_step(repa_total, pieces):
            result, repa_part = stepper(block_weights, pieces[0], pieces[1], pieces[2], pieces[3])
            return (repa_total + repa_part, result)
        sliced = (values.reshape(step_count, group_size, PATCHES, D), per_image.reshape(step_count, group_size, 6 * D), targets.reshape(step_count, group_size, PATCHES, ZDIM), valid_mask.reshape(step_count, group_size))
        repa_total, results = lax.scan(scan_step, jnp.zeros((), jnp.float32), sliced)
        return (results.reshape(IMAGES, PATCHES, D), repa_total)
    primal, pullback = jax.vjp(forward, params, inputs)
    seeds = (cotangent.astype(jnp.float32) * valid_mask[:, None, None], jnp.ones((), jnp.float32))
    grads, grad_input = pullback(seeds)
    return (primal[0].astype(jnp.bfloat16), grad_input, grads[0], grads[1], grads[2], grads[3], grads[4], grads[5], grads[6], grads[7], grads[8], grads[9], grads[10], grads[11])
```

```python
import functools
import math

import jax
import jax.numpy as jnp
from jax import lax
from jax.experimental import pallas as pl
from jax.experimental.pallas import tpu as pltpu
from jax.sharding import PartitionSpec as P

HEADS = 16
ZDIM = 768
FREQ = 256


lambda_repa = 0.5
eps_norm = 1e-06


def normalize(values):
    row_mean = jnp.mean(values, axis=-1, keepdims=True)
    centred = values - row_mean
    return centred * lax.rsqrt(jnp.mean(centred * centred, axis=-1, keepdims=True) + eps_norm)


def modulate(values, scale_vec, shift_vec):
    return normalize(values) * (1.0 + scale_vec) + shift_vec


def multiply(first_op, second_op):
    return jnp.dot(first_op, second_op, preferred_element_type=jnp.float32)


def precise(first_op, second_op):
    return jnp.dot(first_op, second_op.astype(jnp.float32), precision=lax.Precision.HIGHEST)


def contract_rows(first_op, second_op):
    return lax.dot_general(
        first_op, second_op, (((0,), (0,)), ((), ())), preferred_element_type=jnp.float32
    )


def contract_cols(first_op, second_op):
    return lax.dot_general(
        first_op, second_op, (((1,), (1,)), ((), ())), preferred_element_type=jnp.float32
    )


def select_entry(table, index):
    return jnp.sum(jnp.where(jnp.arange(table.shape[0]) == index, table, 0))


def silu_back(inputs, upstream):
    return jax.vjp(jax.nn.silu, inputs)[1](upstream)[0]


def gelu_tanh(values):
    return jax.nn.gelu(values, approximate=True)


def gelu_back(inputs, upstream):
    return jax.vjp(gelu_tanh, inputs)[1](upstream)[0]


NZ = 4
NX = 2


def z_send(values, offset):
    pairs = [(z * NX + x, ((z + offset) % NZ) * NX + x) for z in range(NZ) for x in range(NX)]
    return lax.ppermute(values, "fsdp", pairs)


def x_swap(values):
    return lax.ppermute(values, "fsdp", [(f, f ^ 1) for f in range(NZ * NX)])


def y_swap(values):
    return lax.ppermute(values, "bin", [(b, b ^ 2) for b in range(4)])


def core_swap(values):
    return lax.ppermute(values, "bin", [(b, b ^ 1) for b in range(4)])


def sum_fsdp(values):
    values = values + z_send(values, 1) + z_send(values, 2) + z_send(values, 3)
    return values + x_swap(values)


def order_pair(is_second, mine, other, axis):
    first = jnp.where(is_second, other, mine)
    second = jnp.where(is_second, mine, other)
    return jnp.stack([first, second], axis=axis)


def place_z(parts, z):
    stacked = jnp.stack(parts)
    return jnp.stack(
        [lax.dynamic_index_in_dim(stacked, (z - j) % NZ, 0, False) for j in range(NZ)]
    )


def around_z(values, z):
    return place_z([values] + [z_send(values, r) for r in (1, 2, 3)], z)


class Spot:
    def __init__(self):
        bin_index, fsdp_index = lax.axis_index("bin"), lax.axis_index("fsdp")
        self.y, self.core = bin_index // 2, bin_index % 2
        self.z, self.x = fsdp_index // NX, fsdp_index % NX
        self.fsdp = fsdp_index
        self.bin = bin_index


def gather_small(values, spot):
    column = around_z(values, spot.z)
    both = order_pair(spot.x == 1, column, x_swap(column), 1)
    return both.reshape((NZ * NX,) + values.shape)


class Split:
    def __init__(self, rows, cols, axis, y_width, s_width):
        self.rows, self.cols, self.axis = rows, cols, axis
        self.y_width, self.s_width = y_width, s_width
        self.half = 2 * y_width + s_width
        self.length = (rows, cols)[axis]


def pad_to(values, size, axis):
    extra = size - values.shape[axis]
    if extra == 0:
        return values
    widths = [(0, 0)] * values.ndim
    widths[axis] = (0, extra)
    return jnp.pad(values, widths)


def take(values, start, size, axis):
    return lax.dynamic_slice_in_dim(values, start, size, axis)


def assemble_body(split, *refs):
    sources, out, sems = refs[:12], refs[12], refs[13]
    bin_index = lax.axis_index("bin")
    my_x = lax.rem(lax.axis_index("fsdp"), NX)
    my_y, my_core = bin_index // 2, lax.rem(bin_index, 2)

    def each(action):
        for core in range(2):
            for part in range(3):
                start = core * split.half + part * split.y_width
                width = split.y_width if part < 2 else split.s_width
                width = min(width, split.length - start)
                if width <= 0:
                    continue
                for same_core in (0, 1):
                    for same_y in (0, 1):
                        if part == 2 and not same_y:
                            continue
                        kind = 2 if part == 2 else 1 - same_y
                        cond = my_core == (core if same_core else 1 - core)
                        if part < 2:
                            cond = cond & (my_y == (part if same_y else 1 - part))

                        def run(same_core=same_core, kind=kind, start=start, width=width, core=core, part=part):
                            for other_x in (0, 1):
                                x = 1 - my_x if other_x else my_x
                                src = sources[(1 - same_core) * 6 + kind * 2 + other_x]
                                cut = pl.ds(start, width)
                                if split.axis == 0:
                                    src = src.at[:, pl.ds(0, width), :]
                                    dst = out.at[:, x, cut, :]
                                else:
                                    src = src.at[:, :, pl.ds(0, width)]
                                    dst = out.at[:, x, :, cut]
                                sem = sems.at[core, part, other_x]
                                action(pltpu.make_async_copy(src, dst, sem))

                        pl.when(cond)(run)

    each(lambda copy: copy.start())
    each(lambda copy: copy.wait())


def gather_matrix(shard, split, spot):
    axis = split.axis
    shard = pad_to(shard, 2 * split.half, axis)
    base = spot.core * split.half
    y_piece = take(shard, base + spot.y * split.y_width, split.y_width, axis)
    s_piece = take(shard, base + 2 * split.y_width, split.s_width, axis)
    column = around_z(jnp.concatenate([y_piece, s_piece], axis=axis), spot.z)
    y_own = lax.slice_in_dim(column, 0, split.y_width, axis=axis + 1)
    s_own = lax.slice_in_dim(column, split.y_width, split.y_width + split.s_width, axis=axis + 1)
    y_side, s_side = x_swap(y_own), x_swap(s_own)
    pieces = [y_own, y_side, y_swap(y_own), y_swap(y_side), s_own, s_side]
    pieces = pieces + [core_swap(piece) for piece in pieces]
    out = pl.pallas_call(
        functools.partial(assemble_body, split),
        out_shape=jax.ShapeDtypeStruct((NZ, NX, split.rows, split.cols), shard.dtype),
        in_specs=[pl.BlockSpec(memory_space=pl.ANY)] * 12,
        out_specs=pl.BlockSpec(memory_space=pl.ANY),
        scratch_shapes=[pltpu.SemaphoreType.DMA((2, 3, 2))],
    )(*pieces)
    return out.reshape(NZ * NX * split.rows, split.cols)


def swap_rows(values):
    return jnp.concatenate([values, core_swap(values)], axis=0)


def half_rows(values, width, spot, axis):
    own = take(values, spot.core * width, width, axis)
    sent = take(values, (1 - spot.core) * width, width, axis)
    return jnp.concatenate([own, core_swap(sent)], axis=0)


def scatter_gradient(left, right, split, spot):
    width = split.y_width + split.s_width
    low = jnp.bfloat16
    if split.axis == 1:
        left = swap_rows(left).reshape(-1, NZ, NX, split.rows)
        right = half_rows(pad_to(right, 2 * split.half, 1), split.half, spot, 1)
        side = lax.dynamic_index_in_dim(left, 1 - spot.x, 2, False).reshape(left.shape[0], -1)
        mine = lax.dynamic_index_in_dim(left, spot.x, 2, False).reshape(left.shape[0], -1)
        y_mine = take(right, spot.y * split.y_width, split.y_width, 1)
        y_away = take(right, (1 - spot.y) * split.y_width, split.y_width, 1)
        kept = jnp.concatenate([y_mine, right[:, 2 * split.y_width :]], axis=1)
        away = contract_rows(jnp.concatenate([side, mine], axis=1), y_away).astype(low)
        arrived = pad_to(y_swap(away), width, 1).astype(jnp.float32)
        count = side.shape[1]
        to_side = (contract_rows(side, kept) + arrived[:count]).astype(low)
        total = contract_rows(mine, kept) + arrived[count:]
        total = (total + x_swap(to_side).astype(jnp.float32)).astype(low)
        total = total.reshape(NZ, split.rows, width)
    else:
        left = left.reshape(left.shape[0], NZ * NX, split.rows)
        left = half_rows(left, split.half, spot, 2).reshape(-1, NZ, NX, split.half)
        right = swap_rows(right)
        side = lax.dynamic_index_in_dim(left, 1 - spot.x, 2, False)
        mine = lax.dynamic_index_in_dim(left, spot.x, 2, False)
        deep = left.shape[0]

        def cut(part):
            mid = take(part, spot.y * split.y_width, split.y_width, 2)
            return jnp.concatenate([mid, part[:, :, 2 * split.y_width :]], axis=2)

        def gone(part):
            return take(part, (1 - spot.y) * split.y_width, split.y_width, 2)

        y_left = jnp.stack([gone(side), gone(mine)], axis=1).reshape(deep, -1)
        away = contract_rows(y_left, right).astype(low)
        arrived = y_swap(away).reshape(2, NZ, split.y_width, split.cols)
        arrived = pad_to(arrived, width, 2).astype(jnp.float32).reshape(2, NZ * width, split.cols)
        to_side = (contract_rows(cut(side).reshape(deep, -1), right) + arrived[0]).astype(low)
        total = contract_rows(cut(mine).reshape(deep, -1), right) + arrived[1]
        total = (total + x_swap(to_side).astype(jnp.float32)).astype(low)
        total = total.reshape(NZ, width, split.cols)
    own = lax.dynamic_index_in_dim(total, spot.z, 0, False).astype(jnp.float32)
    for offset in (1, 2, 3):
        sent = lax.dynamic_index_in_dim(total, (spot.z + offset) % NZ, 0, False)
        own = own + z_send(sent, offset).astype(jnp.float32)
    own = own.astype(low)
    axis = split.axis
    other = y_swap(own)
    cut_at = split.y_width
    own_y = lax.slice_in_dim(own, 0, cut_at, axis=axis)
    other_y = lax.slice_in_dim(other, 0, cut_at, axis=axis)
    own_s = lax.slice_in_dim(own, cut_at, width, axis=axis).astype(jnp.float32)
    other_s = lax.slice_in_dim(other, cut_at, width, axis=axis).astype(jnp.float32)
    first = jnp.where(spot.y == 0, own_y, other_y)
    second = jnp.where(spot.y == 0, other_y, own_y)
    half = jnp.concatenate([first, second, (own_s + other_s).astype(low)], axis=axis)
    away_half = core_swap(half)
    whole = jnp.concatenate(
        [
            jnp.where(spot.core == 0, half, away_half),
            jnp.where(spot.core == 0, away_half, half),
        ],
        axis=axis,
    )
    return lax.slice_in_dim(whole, 0, split.length, axis=axis).astype(jnp.float32)


def body(
    tokens,
    features,
    cotangent,
    bin_counts,
    timesteps,
    labels,
    qkv_weight,
    attn_weight,
    up_weight,
    down_weight,
    repa_first,
    repa_second,
    repa_third,
    ada_weight,
    ada_bias,
    time_first,
    time_second,
    label_table,
):
    images, patches, model_width = tokens.shape
    row_count = images * patches
    head_size = model_width // HEADS
    inv_root = 1.0 / math.sqrt(head_size)
    shard_index = lax.axis_index("fsdp")
    bin_index = lax.axis_index("bin")
    image_count = select_entry(bin_counts, bin_index)
    step_value = select_entry(timesteps, bin_index)
    label_value = select_entry(labels, bin_index)
    slots = shard_index * images + jnp.arange(images)
    valid_mask = (slots < image_count).astype(jnp.float32)
    valid_rows = jnp.repeat(valid_mask, patches)
    gathered = (
        lax.all_gather(qkv_weight, "fsdp", axis=0, tiled=True),
        lax.all_gather(attn_weight, "fsdp", axis=0, tiled=True),
        lax.all_gather(up_weight, "fsdp", axis=0, tiled=True),
        lax.all_gather(down_weight, "fsdp", axis=0, tiled=True),
        lax.all_gather(repa_first, "fsdp", axis=0, tiled=True),
        lax.all_gather(repa_second, "fsdp", axis=0, tiled=True),
        lax.all_gather(repa_third, "fsdp", axis=0, tiled=True),
        lax.all_gather(time_first, "fsdp", axis=0, tiled=True),
        lax.all_gather(time_second, "fsdp", axis=0, tiled=True),
    )
    (
        qkv_full,
        attn_full,
        up_full,
        down_full,
        first_full,
        second_full,
        third_full,
        stamp_first,
        stamp_second,
    ) = gathered
    half_freq = FREQ // 2
    frequency = jnp.exp(-math.log(10000.0) * jnp.arange(half_freq, dtype=jnp.float32) / half_freq)
    angles = step_value.astype(jnp.float32) * frequency
    embedded = jnp.concatenate([jnp.cos(angles), jnp.sin(angles)])[None, :]
    time_pre = precise(embedded, stamp_first)
    time_hidden = jax.nn.silu(time_pre)
    onehot = (jnp.arange(label_table.shape[0]) == label_value).astype(jnp.bfloat16)[None, :]
    label_part = multiply(onehot, label_table).astype(jnp.bfloat16)
    label_vec = lax.all_gather(label_part, "fsdp", axis=1, tiled=True)
    condition = precise(time_hidden, stamp_second) + label_vec.astype(jnp.float32)
    cond_act = jax.nn.silu(condition)
    mod_part = precise(cond_act, ada_weight) + ada_bias.astype(jnp.float32)[None, :]
    modulation = lax.all_gather(mod_part, "fsdp", axis=1, tiled=True)[0]
    shift_attn, scale_attn, gate_attn, shift_mlp, scale_mlp, gate_mlp = jnp.split(modulation, 6)
    inputs = tokens.reshape(row_count, model_width).astype(jnp.float32)
    first_in = modulate(inputs, scale_attn, shift_attn).astype(jnp.bfloat16)
    qkv_act = (
        multiply(first_in, qkv_full)
        .astype(jnp.bfloat16)
        .reshape(images, patches, 3, HEADS, head_size)
    )
    query_heads = qkv_act[:, :, 0]
    key_heads = qkv_act[:, :, 1]
    value_heads = qkv_act[:, :, 2]
    scores = (
        jnp.einsum("iqhe,ikhe->ihqk", query_heads, key_heads, preferred_element_type=jnp.float32)
        * inv_root
    )
    row_max = jnp.max(scores, axis=-1, keepdims=True)
    exponent = jnp.exp(scores - row_max)
    exp_total = jnp.sum(exponent, axis=-1, keepdims=True)
    log_total = row_max + jnp.log(exp_total)
    attn_probs = (exponent / exp_total).astype(jnp.bfloat16)
    mixed_heads = jnp.einsum(
        "ihqk,ikhe->iqhe", attn_probs, value_heads, preferred_element_type=jnp.float32
    )
    mixed_heads = mixed_heads.reshape(row_count, model_width).astype(jnp.bfloat16)
    attn_out = multiply(mixed_heads, attn_full)
    middle = inputs + gate_attn * attn_out
    second_in = modulate(middle, scale_mlp, shift_mlp).astype(jnp.bfloat16)
    up_pre = multiply(second_in, up_full)
    up_act = gelu_tanh(up_pre).astype(jnp.bfloat16)
    down_out = multiply(up_act, down_full)
    output_low = (middle + gate_mlp * down_out).astype(jnp.bfloat16)
    first_pre = multiply(output_low, first_full)
    first_act = jax.nn.silu(first_pre).astype(jnp.bfloat16)
    second_pre = multiply(first_act, second_full)
    second_act = jax.nn.silu(second_pre).astype(jnp.bfloat16)
    projected = multiply(second_act, third_full)
    targets = features.reshape(row_count, features.shape[2]).astype(jnp.float32)

    def repa_term(values):
        unit_proj = values * lax.rsqrt(jnp.sum(values * values, axis=-1, keepdims=True) + eps_norm)
        unit_target = targets * lax.rsqrt(
            jnp.sum(targets * targets, axis=-1, keepdims=True) + eps_norm
        )
        return -lambda_repa * ZDIM * jnp.sum(jnp.sum(unit_proj * unit_target, axis=-1) * valid_rows)

    grad_proj = jax.vjp(repa_term, projected)[1](jnp.float32(1.0))[0].astype(jnp.bfloat16)
    regathered = (
        lax.all_gather(qkv_weight, "fsdp", axis=0, tiled=True),
        lax.all_gather(attn_weight, "fsdp", axis=0, tiled=True),
        lax.all_gather(up_weight, "fsdp", axis=0, tiled=True),
        lax.all_gather(down_weight, "fsdp", axis=0, tiled=True),
        lax.all_gather(repa_first, "fsdp", axis=0, tiled=True),
        lax.all_gather(repa_second, "fsdp", axis=0, tiled=True),
        lax.all_gather(repa_third, "fsdp", axis=0, tiled=True),
        lax.all_gather(time_second, "fsdp", axis=0, tiled=True),
    )
    back_qkv, back_attn, back_up, back_down, back_first, back_second, back_third, back_stamp = (
        regathered
    )
    grad_third_full = contract_rows(second_act, grad_proj)
    grad_second_pre = silu_back(second_pre, contract_cols(grad_proj, back_third)).astype(
        jnp.bfloat16
    )
    grad_second_full = contract_rows(first_act, grad_second_pre)
    grad_first_pre = silu_back(first_pre, contract_cols(grad_second_pre, back_second)).astype(
        jnp.bfloat16
    )
    grad_first_full = contract_rows(output_low, grad_first_pre)
    cotangent_rows = (
        cotangent.reshape(row_count, model_width).astype(jnp.float32) * valid_rows[:, None]
    )
    grad_output = contract_cols(grad_first_pre, back_first) + cotangent_rows
    grad_gate_mlp = jnp.sum(grad_output * down_out, axis=0)
    grad_down_in = (gate_mlp * grad_output).astype(jnp.bfloat16)
    grad_down_full = contract_rows(up_act, grad_down_in)
    grad_up_pre = gelu_back(up_pre, contract_cols(grad_down_in, back_down)).astype(jnp.bfloat16)
    grad_up_full = contract_rows(second_in, grad_up_pre)
    middle_pull = jax.vjp(modulate, middle, scale_mlp, shift_mlp)[1]
    grad_middle_norm, grad_scale_mlp, grad_shift_mlp = middle_pull(
        contract_cols(grad_up_pre, back_up)
    )
    grad_middle = grad_output + grad_middle_norm
    grad_gate_attn = jnp.sum(grad_middle * attn_out, axis=0)
    grad_attn_in = (gate_attn * grad_middle).astype(jnp.bfloat16)
    grad_attn_full = contract_rows(mixed_heads, grad_attn_in)
    grad_mixed = (
        contract_cols(grad_attn_in, back_attn)
        .astype(jnp.bfloat16)
        .reshape(images, patches, HEADS, head_size)
    )
    scores_again = (
        jnp.einsum("iqhe,ikhe->ihqk", query_heads, key_heads, preferred_element_type=jnp.float32)
        * inv_root
    )
    probs_again = jnp.exp(scores_again - log_total)
    grad_probs = jnp.einsum(
        "iqhe,ikhe->ihqk", grad_mixed, value_heads, preferred_element_type=jnp.float32
    )
    grad_value = jnp.einsum(
        "ihqk,iqhe->ikhe",
        probs_again.astype(jnp.bfloat16),
        grad_mixed,
        preferred_element_type=jnp.float32,
    )
    row_dots = jnp.sum(grad_probs * probs_again, axis=-1, keepdims=True)
    grad_scores = (probs_again * (grad_probs - row_dots)).astype(jnp.bfloat16)
    grad_query = (
        jnp.einsum("ihqk,ikhe->iqhe", grad_scores, key_heads, preferred_element_type=jnp.float32)
        * inv_root
    )
    grad_key = (
        jnp.einsum("ihqk,iqhe->ikhe", grad_scores, query_heads, preferred_element_type=jnp.float32)
        * inv_root
    )
    grad_qkv_in = (
        jnp.stack([grad_query, grad_key, grad_value], axis=2)
        .astype(jnp.bfloat16)
        .reshape(row_count, 3 * model_width)
    )
    grad_qkv_full = contract_rows(first_in, grad_qkv_in)
    input_pull = jax.vjp(modulate, inputs, scale_attn, shift_attn)[1]
    grad_input_norm, grad_scale_attn, grad_shift_attn = input_pull(
        contract_cols(grad_qkv_in, back_qkv)
    )
    grad_input = grad_middle + grad_input_norm
    grad_modulation = jnp.concatenate(
        [
            grad_shift_attn,
            grad_scale_attn,
            grad_gate_attn,
            grad_shift_mlp,
            grad_scale_mlp,
            grad_gate_mlp,
        ]
    )
    mod_share = lax.psum_scatter(grad_modulation, "fsdp", scatter_dimension=0, tiled=True)
    act_part = jnp.dot(ada_weight.astype(jnp.float32), mod_share, precision=lax.Precision.HIGHEST)
    grad_act = lax.psum(act_part, "fsdp")
    grad_condition = silu_back(condition[0], grad_act)
    col_count = label_table.shape[1]
    grad_cols = lax.dynamic_slice_in_dim(grad_condition, shard_index * col_count, col_count)
    grad_table_part = onehot[0].astype(jnp.float32)[:, None] * grad_cols[None, :]
    row_second = time_second.shape[0]
    hidden_rows = lax.dynamic_slice_in_dim(time_hidden[0], shard_index * row_second, row_second)
    grad_stamp_second = hidden_rows[:, None] * grad_condition[None, :]
    grad_hidden = jnp.dot(
        back_stamp.astype(jnp.float32), grad_condition, precision=lax.Precision.HIGHEST
    )
    grad_time_pre = silu_back(time_pre[0], grad_hidden)
    row_first = time_first.shape[0]
    embed_rows = lax.dynamic_slice_in_dim(embedded[0], shard_index * row_first, row_first)
    grad_stamp_first = embed_rows[:, None] * grad_time_pre[None, :]
    owned = (
        lax.psum_scatter(grad_qkv_full, "fsdp", scatter_dimension=0, tiled=True),
        lax.psum_scatter(grad_attn_full, "fsdp", scatter_dimension=0, tiled=True),
        lax.psum_scatter(grad_up_full, "fsdp", scatter_dimension=0, tiled=True),
        lax.psum_scatter(grad_down_full, "fsdp", scatter_dimension=0, tiled=True),
        lax.psum_scatter(grad_first_full, "fsdp", scatter_dimension=0, tiled=True),
        lax.psum_scatter(grad_second_full, "fsdp", scatter_dimension=0, tiled=True),
        lax.psum_scatter(grad_third_full, "fsdp", scatter_dimension=0, tiled=True),
    )
    own_qkv, own_attn, own_up, own_down, own_first, own_second, own_third = owned
    act_values = cond_act[0]
    all_acts, all_mods = (
        lax.all_gather(act_values, "bin", axis=0, tiled=True),
        lax.all_gather(mod_share, "bin", axis=0, tiled=True),
    )
    bin_total = lax.axis_size("bin")
    acts_matrix = all_acts.reshape(bin_total, act_values.shape[0])
    mods_matrix = all_mods.reshape(bin_total, mod_share.shape[0])
    grad_ada = lax.dot_general(
        acts_matrix, mods_matrix, (((0,), (0,)), ((), ())), precision=lax.Precision.HIGHEST
    )
    grad_bias = jnp.sum(mods_matrix, axis=0)
    summed = lax.psum(
        (
            own_qkv,
            own_attn,
            own_up,
            own_down,
            own_first,
            own_second,
            own_third,
            grad_stamp_first,
            grad_stamp_second,
            grad_table_part,
        ),
        "bin",
    )
    (
        sum_qkv,
        sum_attn,
        sum_up,
        sum_down,
        sum_first,
        sum_second,
        sum_third,
        sum_tfirst,
        sum_tsecond,
        sum_table,
    ) = summed
    return (
        output_low.reshape(images, patches, model_width),
        grad_input.reshape(images, patches, model_width),
        sum_qkv,
        sum_attn,
        sum_up,
        sum_down,
        sum_first,
        sum_second,
        sum_third,
        grad_ada,
        grad_bias,
        sum_tfirst,
        sum_tsecond,
        sum_table,
    )


def torus_body(
    tokens,
    features,
    cotangent,
    bin_counts,
    timesteps,
    labels,
    qkv_weight,
    attn_weight,
    up_weight,
    down_weight,
    repa_first,
    repa_second,
    repa_third,
    ada_weight,
    ada_bias,
    time_first,
    time_second,
    label_table,
):
    images, patches, model_width = tokens.shape
    row_count = images * patches
    head_size = model_width // HEADS
    inv_root = 1.0 / math.sqrt(head_size)
    spot = Spot()
    shard_index, bin_index = spot.fsdp, spot.bin
    image_count = select_entry(bin_counts, bin_index)
    slots = shard_index * images + jnp.arange(images)
    valid_mask = (slots < image_count).astype(jnp.float32)
    valid_rows = jnp.repeat(valid_mask, patches)
    row_first, row_second = time_first.shape[0], time_second.shape[0]
    half_freq = FREQ // 2
    places = shard_index * row_first + jnp.arange(row_first)
    frequency = jnp.exp(
        -math.log(10000.0) * (places % half_freq).astype(jnp.float32) / half_freq
    )
    angles = timesteps.astype(jnp.float32)[:, None] * frequency[None, :]
    embedded = jnp.where(places[None, :] < half_freq, jnp.cos(angles), jnp.sin(angles))
    time_pre = sum_fsdp(precise(embedded, time_first))
    time_hidden = jax.nn.silu(time_pre)
    hidden_rows = take(time_hidden, shard_index * row_second, row_second, 1)
    onehot = (jnp.arange(label_table.shape[0])[None, :] == labels[:, None]).astype(jnp.bfloat16)
    label_part = multiply(onehot, label_table)
    col_count = label_table.shape[1]
    condition_part = precise(hidden_rows, time_second)
    label_full = jnp.zeros_like(condition_part)
    label_full = lax.dynamic_update_slice_in_dim(label_full, label_part, shard_index * col_count, 1)
    condition = sum_fsdp(condition_part + label_full)
    cond_act = jax.nn.silu(condition)
    mod_part = precise(take(cond_act, bin_index, 1, 0), ada_weight)
    mod_part = mod_part[0] + ada_bias.astype(jnp.float32)
    modulation = gather_small(mod_part, spot).reshape(-1)
    shift_attn, scale_attn, gate_attn, shift_mlp, scale_mlp, gate_mlp = jnp.split(modulation, 6)
    splits = {
        "qkv": Split(qkv_weight.shape[0], qkv_weight.shape[1], 1, 640, 512),
        "attn": Split(attn_weight.shape[0], attn_weight.shape[1], 1, 256, 128),
        "up": Split(up_weight.shape[0], up_weight.shape[1], 1, 768, 768),
        "down": Split(down_weight.shape[0], down_weight.shape[1], 0, 96, 96),
        "first": Split(repa_first.shape[0], repa_first.shape[1], 1, 384, 256),
        "second": Split(repa_second.shape[0], repa_second.shape[1], 1, 384, 256),
        "third": Split(repa_third.shape[0], repa_third.shape[1], 1, 128, 128),
    }
    back_splits = {
        "qkv": Split(qkv_weight.shape[0], qkv_weight.shape[1], 1, 512, 768),
        "attn": Split(attn_weight.shape[0], attn_weight.shape[1], 1, 128, 384),
        "up": Split(up_weight.shape[0], up_weight.shape[1], 1, 640, 1024),
        "down": Split(down_weight.shape[0], down_weight.shape[1], 0, 80, 128),
        "first": Split(repa_first.shape[0], repa_first.shape[1], 1, 256, 512),
        "second": Split(repa_second.shape[0], repa_second.shape[1], 1, 256, 512),
        "third": Split(repa_third.shape[0], repa_third.shape[1], 1, 128, 128),
    }
    qkv_full = gather_matrix(qkv_weight, splits["qkv"], spot)
    attn_full = gather_matrix(attn_weight, splits["attn"], spot)
    up_full = gather_matrix(up_weight, splits["up"], spot)
    down_full = gather_matrix(down_weight, splits["down"], spot)
    first_full = gather_matrix(repa_first, splits["first"], spot)
    second_full = gather_matrix(repa_second, splits["second"], spot)
    third_full = gather_matrix(repa_third, splits["third"], spot)
    inputs = tokens.reshape(row_count, model_width).astype(jnp.float32)
    first_in = modulate(inputs, scale_attn, shift_attn).astype(jnp.bfloat16)
    qkv_act = (
        multiply(first_in, qkv_full)
        .astype(jnp.bfloat16)
        .reshape(images, patches, 3, HEADS, head_size)
    )
    query_heads = qkv_act[:, :, 0]
    key_heads = qkv_act[:, :, 1]
    value_heads = qkv_act[:, :, 2]
    scores = (
        jnp.einsum("iqhe,ikhe->ihqk", query_heads, key_heads, preferred_element_type=jnp.float32)
        * inv_root
    )
    row_max = jnp.max(scores, axis=-1, keepdims=True)
    exponent = jnp.exp(scores - row_max)
    exp_total = jnp.sum(exponent, axis=-1, keepdims=True)
    log_total = row_max + jnp.log(exp_total)
    attn_probs = (exponent / exp_total).astype(jnp.bfloat16)
    mixed_heads = jnp.einsum(
        "ihqk,ikhe->iqhe", attn_probs, value_heads, preferred_element_type=jnp.float32
    )
    mixed_heads = mixed_heads.reshape(row_count, model_width).astype(jnp.bfloat16)
    attn_out = multiply(mixed_heads, attn_full)
    middle = inputs + gate_attn * attn_out
    second_in = modulate(middle, scale_mlp, shift_mlp).astype(jnp.bfloat16)
    up_pre = multiply(second_in, up_full)
    up_act = gelu_tanh(up_pre).astype(jnp.bfloat16)
    down_out = multiply(up_act, down_full)
    output_low = (middle + gate_mlp * down_out).astype(jnp.bfloat16)
    first_pre = multiply(output_low, first_full)
    first_act = jax.nn.silu(first_pre).astype(jnp.bfloat16)
    second_pre = multiply(first_act, second_full)
    second_act = jax.nn.silu(second_pre).astype(jnp.bfloat16)
    projected = multiply(second_act, third_full)
    targets = features.reshape(row_count, features.shape[2]).astype(jnp.float32)

    def repa_term(values):
        unit_proj = values * lax.rsqrt(jnp.sum(values * values, axis=-1, keepdims=True) + eps_norm)
        unit_target = targets * lax.rsqrt(
            jnp.sum(targets * targets, axis=-1, keepdims=True) + eps_norm
        )
        return -lambda_repa * ZDIM * jnp.sum(jnp.sum(unit_proj * unit_target, axis=-1) * valid_rows)

    grad_proj = jax.vjp(repa_term, projected)[1](jnp.float32(1.0))[0].astype(jnp.bfloat16)
    sum_third = scatter_gradient(second_act, grad_proj, back_splits["third"], spot)
    grad_second_pre = silu_back(second_pre, contract_cols(grad_proj, third_full)).astype(
        jnp.bfloat16
    )
    sum_second = scatter_gradient(first_act, grad_second_pre, back_splits["second"], spot)
    grad_first_pre = silu_back(first_pre, contract_cols(grad_second_pre, second_full)).astype(
        jnp.bfloat16
    )
    sum_first = scatter_gradient(output_low, grad_first_pre, back_splits["first"], spot)
    cotangent_rows = (
        cotangent.reshape(row_count, model_width).astype(jnp.float32) * valid_rows[:, None]
    )
    grad_output = contract_cols(grad_first_pre, first_full) + cotangent_rows
    grad_gate_mlp = jnp.sum(grad_output * down_out, axis=0)
    grad_down_in = (gate_mlp * grad_output).astype(jnp.bfloat16)
    sum_down = scatter_gradient(up_act, grad_down_in, back_splits["down"], spot)
    grad_up_pre = gelu_back(up_pre, contract_cols(grad_down_in, down_full)).astype(jnp.bfloat16)
    sum_up = scatter_gradient(second_in, grad_up_pre, back_splits["up"], spot)
    middle_pull = jax.vjp(modulate, middle, scale_mlp, shift_mlp)[1]
    grad_middle_norm, grad_scale_mlp, grad_shift_mlp = middle_pull(
        contract_cols(grad_up_pre, up_full)
    )
    grad_middle = grad_output + grad_middle_norm
    grad_gate_attn = jnp.sum(grad_middle * attn_out, axis=0)
    grad_attn_in = (gate_attn * grad_middle).astype(jnp.bfloat16)
    sum_attn = scatter_gradient(mixed_heads, grad_attn_in, back_splits["attn"], spot)
    grad_mixed = (
        contract_cols(grad_attn_in, attn_full)
        .astype(jnp.bfloat16)
        .reshape(images, patches, HEADS, head_size)
    )
    scores_again = (
        jnp.einsum("iqhe,ikhe->ihqk", query_heads, key_heads, preferred_element_type=jnp.float32)
        * inv_root
    )
    probs_again = jnp.exp(scores_again - log_total)
    grad_probs = jnp.einsum(
        "iqhe,ikhe->ihqk", grad_mixed, value_heads, preferred_element_type=jnp.float32
    )
    grad_value = jnp.einsum(
        "ihqk,iqhe->ikhe",
        probs_again.astype(jnp.bfloat16),
        grad_mixed,
        preferred_element_type=jnp.float32,
    )
    row_dots = jnp.sum(grad_probs * probs_again, axis=-1, keepdims=True)
    grad_scores = (probs_again * (grad_probs - row_dots)).astype(jnp.bfloat16)
    grad_query = (
        jnp.einsum("ihqk,ikhe->iqhe", grad_scores, key_heads, preferred_element_type=jnp.float32)
        * inv_root
    )
    grad_key = (
        jnp.einsum("ihqk,iqhe->ikhe", grad_scores, query_heads, preferred_element_type=jnp.float32)
        * inv_root
    )
    grad_qkv_in = (
        jnp.stack([grad_query, grad_key, grad_value], axis=2)
        .astype(jnp.bfloat16)
        .reshape(row_count, 3 * model_width)
    )
    sum_qkv = scatter_gradient(first_in, grad_qkv_in, back_splits["qkv"], spot)
    input_pull = jax.vjp(modulate, inputs, scale_attn, shift_attn)[1]
    grad_input_norm, grad_scale_attn, grad_shift_attn = input_pull(
        contract_cols(grad_qkv_in, qkv_full)
    )
    grad_input = grad_middle + grad_input_norm
    grad_modulation = jnp.concatenate(
        [
            grad_shift_attn,
            grad_scale_attn,
            grad_gate_attn,
            grad_shift_mlp,
            grad_scale_mlp,
            grad_gate_mlp,
        ]
    )
    shares = grad_modulation.reshape(NZ, NX, -1)
    side = lax.dynamic_index_in_dim(shares, 1 - spot.x, 1, False)
    mine = lax.dynamic_index_in_dim(shares, spot.x, 1, False) + x_swap(side)
    mod_share = lax.dynamic_index_in_dim(mine, spot.z, 0, False)
    for offset in (1, 2, 3):
        sent = lax.dynamic_index_in_dim(mine, (spot.z + offset) % NZ, 0, False)
        mod_share = mod_share + z_send(sent, offset)
    core_mods = order_pair(spot.core == 1, mod_share, core_swap(mod_share), 0)
    mods_matrix = order_pair(spot.y == 1, core_mods, y_swap(core_mods), 0).reshape(4, -1)
    act_part = lax.dot_general(
        mods_matrix,
        ada_weight.astype(jnp.float32),
        (((1,), (1,)), ((), ())),
        precision=lax.Precision.HIGHEST,
    )
    grad_condition = silu_back(condition, sum_fsdp(act_part))
    hidden_part = lax.dot_general(
        grad_condition,
        time_second.astype(jnp.float32),
        (((1,), (1,)), ((), ())),
        precision=lax.Precision.HIGHEST,
    )
    grad_hidden = gather_small(hidden_part, spot).transpose(1, 0, 2).reshape(4, -1)
    grad_time_pre = silu_back(time_pre, grad_hidden)

    def outer(left, right):
        return lax.dot_general(
            left, right, (((0,), (0,)), ((), ())), precision=lax.Precision.HIGHEST
        )

    grad_ada = outer(cond_act, mods_matrix)
    grad_bias = jnp.sum(mods_matrix, axis=0)
    sum_tfirst = outer(embedded, grad_time_pre)
    sum_tsecond = outer(hidden_rows, grad_condition)
    grad_cols = take(grad_condition, shard_index * col_count, col_count, 1)
    sum_table = outer(onehot.astype(jnp.float32), grad_cols)
    return (
        output_low.reshape(images, patches, model_width),
        grad_input.reshape(images, patches, model_width),
        sum_qkv,
        sum_attn,
        sum_up,
        sum_down,
        sum_first,
        sum_second,
        sum_third,
        grad_ada,
        grad_bias,
        sum_tfirst,
        sum_tsecond,
        sum_table,
    )


def solution(mesh):
    in_specs = (
        P(("bin", "fsdp"), None, None),
        P(("bin", "fsdp"), None, None),
        P(("bin", "fsdp"), None, None),
        P(),
        P(),
        P(),
        P("fsdp", None),
        P("fsdp", None),
        P("fsdp", None),
        P("fsdp", None),
        P("fsdp", None),
        P("fsdp", None),
        P("fsdp", None),
        P(None, "fsdp"),
        P("fsdp"),
        P("fsdp", None),
        P("fsdp", None),
        P(None, "fsdp"),
    )
    out_specs = (
        P(("bin", "fsdp"), None, None),
        P(("bin", "fsdp"), None, None),
        P("fsdp", None),
        P("fsdp", None),
        P("fsdp", None),
        P("fsdp", None),
        P("fsdp", None),
        P("fsdp", None),
        P("fsdp", None),
        P(None, "fsdp"),
        P("fsdp"),
        P("fsdp", None),
        P("fsdp", None),
        P(None, "fsdp"),
    )
    torus = mesh.shape["bin"] == 4 and mesh.shape["fsdp"] == NZ * NX
    step = torus_body if torus else body
    return jax.shard_map(step, mesh=mesh, in_specs=in_specs, out_specs=out_specs, check_vma=False)
```

```python
import functools
import math

import jax
import jax.numpy as jnp
from jax import lax
from jax.experimental import pallas as pl
from jax.experimental.pallas import tpu as pltpu
from jax.sharding import PartitionSpec as P

HEADS = 16
ZDIM = 768
FREQ = 256


lambda_repa = 0.5
eps_norm = 1e-06


def normalize(values):
    row_mean = jnp.mean(values, axis=-1, keepdims=True)
    centred = values - row_mean
    return centred * lax.rsqrt(jnp.mean(centred * centred, axis=-1, keepdims=True) + eps_norm)


def modulate(values, scale_vec, shift_vec):
    return normalize(values) * (1.0 + scale_vec) + shift_vec


def multiply(first_op, second_op):
    return jnp.dot(first_op, second_op, preferred_element_type=jnp.float32)


def precise(first_op, second_op):
    return jnp.dot(first_op, second_op.astype(jnp.float32), precision=lax.Precision.HIGHEST)


def contract_rows(first_op, second_op):
    return lax.dot_general(
        first_op, second_op, (((0,), (0,)), ((), ())), preferred_element_type=jnp.float32
    )


def contract_cols(first_op, second_op):
    return lax.dot_general(
        first_op, second_op, (((1,), (1,)), ((), ())), preferred_element_type=jnp.float32
    )


def select_entry(table, index):
    return jnp.sum(jnp.where(jnp.arange(table.shape[0]) == index, table, 0))


def silu_back(inputs, upstream):
    return jax.vjp(jax.nn.silu, inputs)[1](upstream)[0]


def gelu_tanh(values):
    return jax.nn.gelu(values, approximate=True)


def gelu_back(inputs, upstream):
    return jax.vjp(gelu_tanh, inputs)[1](upstream)[0]


NZ = 4
NX = 2


def z_send(values, offset):
    pairs = [(z * NX + x, ((z + offset) % NZ) * NX + x) for z in range(NZ) for x in range(NX)]
    return lax.ppermute(values, "fsdp", pairs)


def x_swap(values):
    return lax.ppermute(values, "fsdp", [(f, f ^ 1) for f in range(NZ * NX)])


def y_swap(values):
    return lax.ppermute(values, "bin", [(b, b ^ 2) for b in range(4)])


def core_swap(values):
    return lax.ppermute(values, "bin", [(b, b ^ 1) for b in range(4)])


def sum_fsdp(values):
    values = values + z_send(values, 1) + z_send(values, 2) + z_send(values, 3)
    return values + x_swap(values)


def order_pair(is_second, mine, other, axis):
    first = jnp.where(is_second, other, mine)
    second = jnp.where(is_second, mine, other)
    return jnp.stack([first, second], axis=axis)


def place_z(parts, z):
    stacked = jnp.stack(parts)
    return jnp.stack(
        [lax.dynamic_index_in_dim(stacked, (z - j) % NZ, 0, False) for j in range(NZ)]
    )


def around_z(values, z):
    return place_z([values] + [z_send(values, r) for r in (1, 2, 3)], z)


class Spot:
    def __init__(self):
        bin_index, fsdp_index = lax.axis_index("bin"), lax.axis_index("fsdp")
        self.y, self.core = bin_index // 2, bin_index % 2
        self.z, self.x = fsdp_index // NX, fsdp_index % NX
        self.fsdp = fsdp_index
        self.bin = bin_index


def gather_small(values, spot):
    column = around_z(values, spot.z)
    both = order_pair(spot.x == 1, column, x_swap(column), 1)
    return both.reshape((NZ * NX,) + values.shape)


class Split:
    def __init__(self, rows, cols, axis, y_width, s_width):
        self.rows, self.cols, self.axis = rows, cols, axis
        self.y_width, self.s_width = y_width, s_width
        self.half = 2 * y_width + s_width
        self.length = (rows, cols)[axis]


def pad_to(values, size, axis):
    extra = size - values.shape[axis]
    if extra == 0:
        return values
    widths = [(0, 0)] * values.ndim
    widths[axis] = (0, extra)
    return jnp.pad(values, widths)


def take(values, start, size, axis):
    return lax.dynamic_slice_in_dim(values, start, size, axis)


def hbm_call(body, inputs, out_shapes, sems):
    return pl.pallas_call(
        body,
        out_shape=out_shapes,
        in_specs=[pl.BlockSpec(memory_space=pl.ANY)] * len(inputs),
        out_specs=[pl.BlockSpec(memory_space=pltpu.VMEM)] * len(out_shapes),
        scratch_shapes=[pltpu.SemaphoreType.DMA((sems,))],
        compiler_params=pltpu.CompilerParams(vmem_limit_bytes=28 * 1024 * 1024),
    )(*inputs)


def z_exchange(values):
    groups = [[z * NX + x for z in range(NZ)] for x in range(NX)]
    return lax.all_to_all(values, "fsdp", 0, 0, axis_index_groups=groups, tiled=True)


def half_body(split, *refs):
    near, side, far, out, sems = refs
    fsdp_index = lax.axis_index("fsdp")
    x, z = lax.rem(fsdp_index, NX), fsdp_index // NX
    y = lax.axis_index("bin") // 2
    wide = split.y_width
    copies = []
    for own, ref in enumerate((near, side)):
        at_x = x if own == 0 else 1 - x
        for r in range(NZ):
            at_z = lax.rem(z + NZ - r, NZ)
            for src, first, start, width in (
                (ref.at[r], 0, y * wide, wide),
                (far.at[own, r], 0, (1 - y) * wide, wide),
                (ref.at[r], wide, 2 * wide, split.s_width),
            ):
                cut = pl.ds(pl.multiple_of(start, 128 if split.axis else 16), width)
                if split.axis == 0:
                    piece, dst = src.at[pl.ds(first, width), :], out.at[at_z, at_x, cut, :]
                else:
                    piece, dst = src.at[:, pl.ds(first, width)], out.at[at_z, at_x, :, cut]
                copies.append(pltpu.make_async_copy(piece, dst, sems.at[len(copies)]))
    for copy in copies:
        copy.start()
    for copy in copies:
        copy.wait()


def whole_body(splits, *refs):
    n = len(splits)
    mine, others, out, sems = refs[:n], refs[n : 2 * n], refs[2 * n], refs[2 * n + 1]
    core = lax.rem(lax.axis_index("bin"), 2)

    def each(action):
        half = sum(split.half for split in splits)
        for side in range(2):
            start = side * half
            for k, split in enumerate(splits):
                width = min(split.half, split.length - start)
                for own in (0, 1):

                    def run(own=own, start=start, width=width, k=k, side=side):
                        ref = mine[k] if own else others[k]
                        if split.axis == 0:
                            src = ref.at[:, :, pl.ds(0, width), :]
                            dst = out.at[:, :, pl.ds(start, width), :]
                        else:
                            src = ref.at[:, :, :, pl.ds(0, width)]
                            dst = out.at[:, :, :, pl.ds(start, width)]
                        action(pltpu.make_async_copy(src, dst, sems.at[side * n + k]))

                    pl.when(core == (side if own else 1 - side))(run)
                start += width

    each(lambda copy: copy.start())
    each(lambda copy: copy.wait())


def dot_rows(first_op, second_op):
    return lax.dot_general(
        first_op, second_op, (((1,), (1,)), ((), ())), preferred_element_type=jnp.float32
    )


def head_probs(query, key, inv_root):
    scores = dot_rows(query, key) * inv_root
    exponent = jnp.exp(scores - jnp.max(scores, axis=-1, keepdims=True))
    return exponent / jnp.sum(exponent, axis=-1, keepdims=True)


def attention_body(qkv_ref, out_ref):
    width = out_ref.shape[1]
    size = width // HEADS
    for head in range(HEADS):
        cut = slice(head * size, (head + 1) * size)
        query = qkv_ref[:, cut]
        key = qkv_ref[:, width + cut.start : width + cut.stop]
        value = qkv_ref[:, 2 * width + cut.start : 2 * width + cut.stop]
        probs = head_probs(query, key, size**-0.5).astype(jnp.bfloat16)
        mixed = jnp.dot(probs, value, preferred_element_type=jnp.float32)
        out_ref[:, cut] = mixed.astype(jnp.bfloat16)


def attention(qkv, patches):
    rows, width = qkv.shape[0], qkv.shape[1] // 3
    return pl.pallas_call(
        attention_body,
        grid=(rows // patches,),
        out_shape=jax.ShapeDtypeStruct((rows, width), jnp.bfloat16),
        in_specs=[pl.BlockSpec((patches, 3 * width), lambda i: (i, 0))],
        out_specs=pl.BlockSpec((patches, width), lambda i: (i, 0)),
        compiler_params=pltpu.CompilerParams(vmem_limit_bytes=32 * 1024 * 1024),
    )(qkv)


def attention_back_body(qkv_ref, grad_ref, out_ref):
    width = grad_ref.shape[1]
    size = width // HEADS
    inv_root = size**-0.5
    low = jnp.bfloat16
    for head in range(HEADS):
        cuts = [slice(k * width + head * size, k * width + (head + 1) * size) for k in range(3)]
        query, key, value = [qkv_ref[:, cut] for cut in cuts]
        grad = grad_ref[:, cuts[0]]
        probs = head_probs(query, key, inv_root)
        grad_probs = dot_rows(grad, value)
        inner = jnp.sum(grad_probs * probs, axis=-1, keepdims=True)
        grad_scores = (probs * (grad_probs - inner)).astype(low)
        grad_query = jnp.dot(grad_scores, key, preferred_element_type=jnp.float32) * inv_root
        over_rows = (((0,), (0,)), ((), ()))
        grad_key = lax.dot_general(
            grad_scores, query, over_rows, preferred_element_type=jnp.float32
        )
        grad_value = lax.dot_general(
            probs.astype(low), grad, over_rows, preferred_element_type=jnp.float32
        )
        out_ref[:, cuts[0]] = grad_query.astype(low)
        out_ref[:, cuts[1]] = (grad_key * inv_root).astype(low)
        out_ref[:, cuts[2]] = grad_value.astype(low)


def attention_back(qkv, grad, patches):
    rows, width = grad.shape
    return pl.pallas_call(
        attention_back_body,
        grid=(rows // patches,),
        out_shape=jax.ShapeDtypeStruct((rows, 3 * width), jnp.bfloat16),
        in_specs=[
            pl.BlockSpec((patches, 3 * width), lambda i: (i, 0)),
            pl.BlockSpec((patches, width), lambda i: (i, 0)),
        ],
        out_specs=pl.BlockSpec((patches, 3 * width), lambda i: (i, 0)),
        compiler_params=pltpu.CompilerParams(vmem_limit_bytes=32 * 1024 * 1024),
    )(qkv, grad)


class Board:
    def __init__(self):
        self.flows, self.results, self.fresh = {}, {}, {}

    def start(self, name, flow):
        self.fresh[name] = flow

    def run(self):
        waiting = {}
        while self.flows or self.fresh:
            self.flows.update(self.fresh)
            waiting.update({name: None for name in self.fresh})
            self.fresh = {}
            for name in list(self.flows):
                try:
                    waiting[name] = self.flows[name].send(waiting[name])
                except StopIteration as stop:
                    self.results[name] = stop.value
                    del self.flows[name], waiting[name]
            done = lax.optimization_barrier(list(waiting.values()))
            waiting = dict(zip(waiting, done))


def later(steps, flow):
    for _ in range(steps):
        yield ()
    return (yield from flow)


def all_of(board, names):
    while any(name not in board.results for name in names):
        yield ()
    return [board.results[name] for name in names]


def gather_chunk(shard, split, start, half, spot):
    axis = split.axis
    base = spot.core * half + start
    y_piece = take(shard, base + spot.y * split.y_width, split.y_width, axis)
    s_piece = take(shard, base + 2 * split.y_width, split.s_width, axis)
    piece = jnp.concatenate([y_piece, s_piece], axis=axis)
    pieces = yield [piece] + [z_send(piece, r) for r in (1, 2, 3)]
    near = jnp.stack(pieces)
    near, side = yield near, x_swap(near)
    both = [lax.slice_in_dim(part, 0, split.y_width, axis=axis + 1) for part in (near, side)]
    near, side, far = yield near, side, y_swap(jnp.stack(both))
    shape = [split.rows, split.cols]
    shape[axis] = split.half
    (mine,) = hbm_call(
        functools.partial(half_body, split),
        [near, side, far],
        [jax.ShapeDtypeStruct((NZ, NX, *shape), near.dtype)],
        6 * NZ,
    )
    return (yield mine, core_swap(mine))


def whole_matrix(splits, halves):
    rows, cols = splits[0].rows, splits[0].cols
    (out,) = hbm_call(
        functools.partial(whole_body, splits),
        [half for half, _ in halves] + [other for _, other in halves],
        [jax.ShapeDtypeStruct((NZ, NX, rows, cols), halves[0][0].dtype)],
        2 * len(splits),
    )
    return out.reshape(NZ * NX * rows, cols)


def scatter_chunk(left, right, split, start, half, spot):
    width = split.y_width + split.s_width
    low, deep = jnp.bfloat16, jnp.float32
    base = spot.core * half + start
    y_away = take(right, base + (1 - spot.y) * split.y_width, split.y_width, 1)
    y_mine = take(right, base + spot.y * split.y_width, split.y_width, 1)
    shared = take(right, base + 2 * split.y_width, split.s_width, 1)
    away = contract_rows(left, y_away).astype(low)
    kept = contract_rows(left, jnp.concatenate([y_mine, shared], axis=1)).astype(low)
    kept, arrived = yield kept, y_swap(away)
    kept = kept.reshape(NZ, NX, split.rows, width)
    arrived = arrived.reshape(NZ, NX, split.rows, split.y_width)


    def along_x(index):
        part = lax.dynamic_index_in_dim(kept, index, 1, False).astype(deep)
        extra = lax.dynamic_index_in_dim(arrived, index, 1, False).astype(deep)
        return (part + pad_to(extra, width, 2)).astype(low)

    kept, arrived, side = yield kept, arrived, x_swap(along_x(1 - spot.x))

    def share(r):
        z = (spot.z + r) % NZ
        part = lax.dynamic_slice(kept, (z, spot.x, 0, 0), (1, 1, split.rows, width))
        extra = lax.dynamic_slice(arrived, (z, spot.x, 0, 0), (1, 1, split.rows, split.y_width))
        extra = pad_to(extra[0, 0].astype(deep), width, 1)
        other = lax.dynamic_index_in_dim(side, z, 0, False).astype(deep)
        return (part[0, 0].astype(deep) + extra + other).astype(low)

    shares = yield [share(0)] + [z_send(share(r), r) for r in (1, 2, 3)]
    own = sum(part.astype(deep) for part in shares).astype(low)
    own, other = yield own, y_swap(own)
    return (yield own, other, core_swap(own), core_swap(other))


def shard_body(splits, *refs):
    n, out = len(splits), refs[-1]
    bin_index = lax.axis_index("bin")
    my_y, my_core = bin_index // 2, lax.rem(bin_index, 2)
    half = sum(split.half for split in splits)

    def put(start, value):
        width = min(value.shape[1], out.shape[1] - start)
        if width > 0:
            out[:, start : start + width] = value[:, :width]

    def fill(core, y):
        for side in range(2):
            start = side * half
            for k, split in enumerate(splits):
                pair = refs[4 * k : 4 * k + 2] if side == core else refs[4 * k + 2 : 4 * k + 4]
                own, other = [ref[...].astype(jnp.float32) for ref in pair]
                wide = split.y_width
                put(start + y * wide, own[:, :wide])
                put(start + (1 - y) * wide, other[:, :wide])
                if split.s_width:
                    put(start + 2 * wide, own[:, wide:] + other[:, wide:])
                start += split.half

    for core in range(2):
        for y in range(2):
            pl.when((my_core == core) & (my_y == y))(functools.partial(fill, core, y))


def whole_gradient(splits, parts, cols):
    inputs = [part for chunk in parts for part in chunk]
    return pl.pallas_call(
        functools.partial(shard_body, splits),
        out_shape=jax.ShapeDtypeStruct((splits[0].rows, cols), jnp.float32),
        compiler_params=pltpu.CompilerParams(vmem_limit_bytes=32 * 1024 * 1024),
    )(*inputs)


def body(
    tokens,
    features,
    cotangent,
    bin_counts,
    timesteps,
    labels,
    qkv_weight,
    attn_weight,
    up_weight,
    down_weight,
    repa_first,
    repa_second,
    repa_third,
    ada_weight,
    ada_bias,
    time_first,
    time_second,
    label_table,
):
    images, patches, model_width = tokens.shape
    row_count = images * patches
    head_size = model_width // HEADS
    inv_root = 1.0 / math.sqrt(head_size)
    shard_index = lax.axis_index("fsdp")
    bin_index = lax.axis_index("bin")
    image_count = select_entry(bin_counts, bin_index)
    step_value = select_entry(timesteps, bin_index)
    label_value = select_entry(labels, bin_index)
    slots = shard_index * images + jnp.arange(images)
    valid_mask = (slots < image_count).astype(jnp.float32)
    valid_rows = jnp.repeat(valid_mask, patches)
    gathered = (
        lax.all_gather(qkv_weight, "fsdp", axis=0, tiled=True),
        lax.all_gather(attn_weight, "fsdp", axis=0, tiled=True),
        lax.all_gather(up_weight, "fsdp", axis=0, tiled=True),
        lax.all_gather(down_weight, "fsdp", axis=0, tiled=True),
        lax.all_gather(repa_first, "fsdp", axis=0, tiled=True),
        lax.all_gather(repa_second, "fsdp", axis=0, tiled=True),
        lax.all_gather(repa_third, "fsdp", axis=0, tiled=True),
        lax.all_gather(time_first, "fsdp", axis=0, tiled=True),
        lax.all_gather(time_second, "fsdp", axis=0, tiled=True),
    )
    (
        qkv_full,
        attn_full,
        up_full,
        down_full,
        first_full,
        second_full,
        third_full,
        stamp_first,
        stamp_second,
    ) = gathered
    half_freq = FREQ // 2
    frequency = jnp.exp(-math.log(10000.0) * jnp.arange(half_freq, dtype=jnp.float32) / half_freq)
    angles = step_value.astype(jnp.float32) * frequency
    embedded = jnp.concatenate([jnp.cos(angles), jnp.sin(angles)])[None, :]
    time_pre = precise(embedded, stamp_first)
    time_hidden = jax.nn.silu(time_pre)
    onehot = (jnp.arange(label_table.shape[0]) == label_value).astype(jnp.bfloat16)[None, :]
    label_part = multiply(onehot, label_table).astype(jnp.bfloat16)
    label_vec = lax.all_gather(label_part, "fsdp", axis=1, tiled=True)
    condition = precise(time_hidden, stamp_second) + label_vec.astype(jnp.float32)
    cond_act = jax.nn.silu(condition)
    mod_part = precise(cond_act, ada_weight) + ada_bias.astype(jnp.float32)[None, :]
    modulation = lax.all_gather(mod_part, "fsdp", axis=1, tiled=True)[0]
    shift_attn, scale_attn, gate_attn, shift_mlp, scale_mlp, gate_mlp = jnp.split(modulation, 6)
    inputs = tokens.reshape(row_count, model_width).astype(jnp.float32)
    first_in = modulate(inputs, scale_attn, shift_attn).astype(jnp.bfloat16)
    qkv_act = (
        multiply(first_in, qkv_full)
        .astype(jnp.bfloat16)
        .reshape(images, patches, 3, HEADS, head_size)
    )
    query_heads = qkv_act[:, :, 0]
    key_heads = qkv_act[:, :, 1]
    value_heads = qkv_act[:, :, 2]
    scores = (
        jnp.einsum("iqhe,ikhe->ihqk", query_heads, key_heads, preferred_element_type=jnp.float32)
        * inv_root
    )
    row_max = jnp.max(scores, axis=-1, keepdims=True)
    exponent = jnp.exp(scores - row_max)
    exp_total = jnp.sum(exponent, axis=-1, keepdims=True)
    log_total = row_max + jnp.log(exp_total)
    attn_probs = (exponent / exp_total).astype(jnp.bfloat16)
    mixed_heads = jnp.einsum(
        "ihqk,ikhe->iqhe", attn_probs, value_heads, preferred_element_type=jnp.float32
    )
    mixed_heads = mixed_heads.reshape(row_count, model_width).astype(jnp.bfloat16)
    attn_out = multiply(mixed_heads, attn_full)
    middle = inputs + gate_attn * attn_out
    second_in = modulate(middle, scale_mlp, shift_mlp).astype(jnp.bfloat16)
    up_pre = multiply(second_in, up_full)
    up_act = gelu_tanh(up_pre).astype(jnp.bfloat16)
    down_out = multiply(up_act, down_full)
    output_low = (middle + gate_mlp * down_out).astype(jnp.bfloat16)
    first_pre = multiply(output_low, first_full)
    first_act = jax.nn.silu(first_pre).astype(jnp.bfloat16)
    second_pre = multiply(first_act, second_full)
    second_act = jax.nn.silu(second_pre).astype(jnp.bfloat16)
    projected = multiply(second_act, third_full)
    targets = features.reshape(row_count, features.shape[2]).astype(jnp.float32)

    def repa_term(values):
        unit_proj = values * lax.rsqrt(jnp.sum(values * values, axis=-1, keepdims=True) + eps_norm)
        unit_target = targets * lax.rsqrt(
            jnp.sum(targets * targets, axis=-1, keepdims=True) + eps_norm
        )
        return -lambda_repa * ZDIM * jnp.sum(jnp.sum(unit_proj * unit_target, axis=-1) * valid_rows)

    grad_proj = jax.vjp(repa_term, projected)[1](jnp.float32(1.0))[0].astype(jnp.bfloat16)
    regathered = (
        lax.all_gather(qkv_weight, "fsdp", axis=0, tiled=True),
        lax.all_gather(attn_weight, "fsdp", axis=0, tiled=True),
        lax.all_gather(up_weight, "fsdp", axis=0, tiled=True),
        lax.all_gather(down_weight, "fsdp", axis=0, tiled=True),
        lax.all_gather(repa_first, "fsdp", axis=0, tiled=True),
        lax.all_gather(repa_second, "fsdp", axis=0, tiled=True),
        lax.all_gather(repa_third, "fsdp", axis=0, tiled=True),
        lax.all_gather(time_second, "fsdp", axis=0, tiled=True),
    )
    back_qkv, back_attn, back_up, back_down, back_first, back_second, back_third, back_stamp = (
        regathered
    )
    grad_third_full = contract_rows(second_act, grad_proj)
    grad_second_pre = silu_back(second_pre, contract_cols(grad_proj, back_third)).astype(
        jnp.bfloat16
    )
    grad_second_full = contract_rows(first_act, grad_second_pre)
    grad_first_pre = silu_back(first_pre, contract_cols(grad_second_pre, back_second)).astype(
        jnp.bfloat16
    )
    grad_first_full = contract_rows(output_low, grad_first_pre)
    cotangent_rows = (
        cotangent.reshape(row_count, model_width).astype(jnp.float32) * valid_rows[:, None]
    )
    grad_output = contract_cols(grad_first_pre, back_first) + cotangent_rows
    grad_gate_mlp = jnp.sum(grad_output * down_out, axis=0)
    grad_down_in = (gate_mlp * grad_output).astype(jnp.bfloat16)
    grad_down_full = contract_rows(up_act, grad_down_in)
    grad_up_pre = gelu_back(up_pre, contract_cols(grad_down_in, back_down)).astype(jnp.bfloat16)
    grad_up_full = contract_rows(second_in, grad_up_pre)
    middle_pull = jax.vjp(modulate, middle, scale_mlp, shift_mlp)[1]
    grad_middle_norm, grad_scale_mlp, grad_shift_mlp = middle_pull(
        contract_cols(grad_up_pre, back_up)
    )
    grad_middle = grad_output + grad_middle_norm
    grad_gate_attn = jnp.sum(grad_middle * attn_out, axis=0)
    grad_attn_in = (gate_attn * grad_middle).astype(jnp.bfloat16)
    grad_attn_full = contract_rows(mixed_heads, grad_attn_in)
    grad_mixed = (
        contract_cols(grad_attn_in, back_attn)
        .astype(jnp.bfloat16)
        .reshape(images, patches, HEADS, head_size)
    )
    scores_again = (
        jnp.einsum("iqhe,ikhe->ihqk", query_heads, key_heads, preferred_element_type=jnp.float32)
        * inv_root
    )
    probs_again = jnp.exp(scores_again - log_total)
    grad_probs = jnp.einsum(
        "iqhe,ikhe->ihqk", grad_mixed, value_heads, preferred_element_type=jnp.float32
    )
    grad_value = jnp.einsum(
        "ihqk,iqhe->ikhe",
        probs_again.astype(jnp.bfloat16),
        grad_mixed,
        preferred_element_type=jnp.float32,
    )
    row_dots = jnp.sum(grad_probs * probs_again, axis=-1, keepdims=True)
    grad_scores = (probs_again * (grad_probs - row_dots)).astype(jnp.bfloat16)
    grad_query = (
        jnp.einsum("ihqk,ikhe->iqhe", grad_scores, key_heads, preferred_element_type=jnp.float32)
        * inv_root
    )
    grad_key = (
        jnp.einsum("ihqk,iqhe->ikhe", grad_scores, query_heads, preferred_element_type=jnp.float32)
        * inv_root
    )
    grad_qkv_in = (
        jnp.stack([grad_query, grad_key, grad_value], axis=2)
        .astype(jnp.bfloat16)
        .reshape(row_count, 3 * model_width)
    )
    grad_qkv_full = contract_rows(first_in, grad_qkv_in)
    input_pull = jax.vjp(modulate, inputs, scale_attn, shift_attn)[1]
    grad_input_norm, grad_scale_attn, grad_shift_attn = input_pull(
        contract_cols(grad_qkv_in, back_qkv)
    )
    grad_input = grad_middle + grad_input_norm
    grad_modulation = jnp.concatenate(
        [
            grad_shift_attn,
            grad_scale_attn,
            grad_gate_attn,
            grad_shift_mlp,
            grad_scale_mlp,
            grad_gate_mlp,
        ]
    )
    mod_share = lax.psum_scatter(grad_modulation, "fsdp", scatter_dimension=0, tiled=True)
    act_part = jnp.dot(ada_weight.astype(jnp.float32), mod_share, precision=lax.Precision.HIGHEST)
    grad_act = lax.psum(act_part, "fsdp")
    grad_condition = silu_back(condition[0], grad_act)
    col_count = label_table.shape[1]
    grad_cols = lax.dynamic_slice_in_dim(grad_condition, shard_index * col_count, col_count)
    grad_table_part = onehot[0].astype(jnp.float32)[:, None] * grad_cols[None, :]
    row_second = time_second.shape[0]
    hidden_rows = lax.dynamic_slice_in_dim(time_hidden[0], shard_index * row_second, row_second)
    grad_stamp_second = hidden_rows[:, None] * grad_condition[None, :]
    grad_hidden = jnp.dot(
        back_stamp.astype(jnp.float32), grad_condition, precision=lax.Precision.HIGHEST
    )
    grad_time_pre = silu_back(time_pre[0], grad_hidden)
    row_first = time_first.shape[0]
    embed_rows = lax.dynamic_slice_in_dim(embedded[0], shard_index * row_first, row_first)
    grad_stamp_first = embed_rows[:, None] * grad_time_pre[None, :]
    owned = (
        lax.psum_scatter(grad_qkv_full, "fsdp", scatter_dimension=0, tiled=True),
        lax.psum_scatter(grad_attn_full, "fsdp", scatter_dimension=0, tiled=True),
        lax.psum_scatter(grad_up_full, "fsdp", scatter_dimension=0, tiled=True),
        lax.psum_scatter(grad_down_full, "fsdp", scatter_dimension=0, tiled=True),
        lax.psum_scatter(grad_first_full, "fsdp", scatter_dimension=0, tiled=True),
        lax.psum_scatter(grad_second_full, "fsdp", scatter_dimension=0, tiled=True),
        lax.psum_scatter(grad_third_full, "fsdp", scatter_dimension=0, tiled=True),
    )
    own_qkv, own_attn, own_up, own_down, own_first, own_second, own_third = owned
    act_values = cond_act[0]
    all_acts, all_mods = (
        lax.all_gather(act_values, "bin", axis=0, tiled=True),
        lax.all_gather(mod_share, "bin", axis=0, tiled=True),
    )
    bin_total = lax.axis_size("bin")
    acts_matrix = all_acts.reshape(bin_total, act_values.shape[0])
    mods_matrix = all_mods.reshape(bin_total, mod_share.shape[0])
    grad_ada = lax.dot_general(
        acts_matrix, mods_matrix, (((0,), (0,)), ((), ())), precision=lax.Precision.HIGHEST
    )
    grad_bias = jnp.sum(mods_matrix, axis=0)
    summed = lax.psum(
        (
            own_qkv,
            own_attn,
            own_up,
            own_down,
            own_first,
            own_second,
            own_third,
            grad_stamp_first,
            grad_stamp_second,
            grad_table_part,
        ),
        "bin",
    )
    (
        sum_qkv,
        sum_attn,
        sum_up,
        sum_down,
        sum_first,
        sum_second,
        sum_third,
        sum_tfirst,
        sum_tsecond,
        sum_table,
    ) = summed
    return (
        output_low.reshape(images, patches, model_width),
        grad_input.reshape(images, patches, model_width),
        sum_qkv,
        sum_attn,
        sum_up,
        sum_down,
        sum_first,
        sum_second,
        sum_third,
        grad_ada,
        grad_bias,
        sum_tfirst,
        sum_tsecond,
        sum_table,
    )


def torus_body(
    tokens,
    features,
    cotangent,
    bin_counts,
    timesteps,
    labels,
    qkv_weight,
    attn_weight,
    up_weight,
    down_weight,
    repa_first,
    repa_second,
    repa_third,
    ada_weight,
    ada_bias,
    time_first,
    time_second,
    label_table,
):
    images, patches, model_width = tokens.shape
    row_count = images * patches
    spot = Spot()
    shard_index, bin_index = spot.fsdp, spot.bin
    image_count = select_entry(bin_counts, bin_index)
    slots = shard_index * images + jnp.arange(images)
    valid_mask = (slots < image_count).astype(jnp.float32)
    valid_rows = jnp.repeat(valid_mask, patches)
    row_first, row_second = time_first.shape[0], time_second.shape[0]
    half_freq = FREQ // 2
    places = shard_index * row_first + jnp.arange(row_first)
    frequency = jnp.exp(
        -math.log(10000.0) * (places % half_freq).astype(jnp.float32) / half_freq
    )
    angles = timesteps.astype(jnp.float32)[:, None] * frequency[None, :]
    embedded = jnp.where(places[None, :] < half_freq, jnp.cos(angles), jnp.sin(angles))
    time_pre = sum_fsdp(precise(embedded, time_first))
    time_hidden = jax.nn.silu(time_pre)
    hidden_rows = take(time_hidden, shard_index * row_second, row_second, 1)
    onehot = (jnp.arange(label_table.shape[0])[None, :] == labels[:, None]).astype(jnp.bfloat16)
    label_part = multiply(onehot, label_table)
    col_count = label_table.shape[1]
    condition_part = precise(hidden_rows, time_second)
    label_full = jnp.zeros_like(condition_part)
    label_full = lax.dynamic_update_slice_in_dim(label_full, label_part, shard_index * col_count, 1)
    condition = sum_fsdp(condition_part + label_full)
    cond_act = jax.nn.silu(condition)
    mod_part = precise(take(cond_act, bin_index, 1, 0), ada_weight)
    mod_part = mod_part[0] + ada_bias.astype(jnp.float32)
    modulation = gather_small(mod_part, spot).reshape(-1)
    shift_attn, scale_attn, gate_attn, shift_mlp, scale_mlp, gate_mlp = jnp.split(modulation, 6)


    board = Board()
    order = [
        ("qkv", qkv_weight, 1, ((640, 512),)),
        ("attn", attn_weight, 1, ((256, 128),)),
        ("up", up_weight, 1, ((384, 384), (384, 384))),
        ("down", down_weight, 0, ((48, 48), (48, 48))),
        ("first", repa_first, 1, ((384, 256),)),
        ("second", repa_second, 1, ((384, 256),)),
        ("third", repa_third, 1, ((128, 128),)),
    ]
    chunk_names, chunk_splits, count = {}, {}, 0
    for name, shard, axis, pairs in order:
        splits = [Split(shard.shape[0], shard.shape[1], axis, *pair) for pair in pairs]
        half = sum(split.half for split in splits)
        padded = pad_to(shard, 2 * half, axis)
        chunk_names[name], chunk_splits[name], start = [], splits, 0
        for k, split in enumerate(splits):
            flow = gather_chunk(padded, split, start, half, spot)
            board.start((name, k), later(count, flow))
            chunk_names[name].append((name, k))
            start += split.half
            count += 1

    def whole(name):
        halves = yield from all_of(board, chunk_names[name])
        return whole_matrix(chunk_splits[name], halves)

    back_pairs = {
        "qkv": ((256, 384), (256, 384)),
        "attn": ((128, 384),),
        "up": ((640, 1024),),
        "down": ((128, 384),),
        "first": ((256, 512),),
        "second": ((256, 512),),
        "third": ((128, 128),),
    }
    shapes = {name: (shard.shape[0], shard.shape[1]) for name, shard, _, _ in order}
    grad_names = {}

    def give(name, left, right):
        splits = [Split(*shapes[name], 1, *pair) for pair in back_pairs[name]]
        half = sum(split.half for split in splits)
        left = jnp.concatenate(left, axis=0)
        right = [pad_to(part, 2 * half, 1) for part in right]
        right = jnp.concatenate(right, axis=0)
        grad_names[name], start = [], 0
        for k, split in enumerate(splits):
            flow = scatter_chunk(left, right, split, start, half, spot)
            board.start(("grad", name, k), later(k, flow))
            grad_names[name].append(("grad", name, k))
            start += split.half

    def compute():
        inputs = tokens.reshape(row_count, model_width).astype(jnp.float32)
        first_in = modulate(inputs, scale_attn, shift_attn).astype(jnp.bfloat16)
        qkv_full = yield from whole("qkv")
        qkv_act = multiply(first_in, qkv_full).astype(jnp.bfloat16)
        qkv_act, first_in, first_in_far = yield qkv_act, first_in, core_swap(first_in)
        mixed_heads = attention(qkv_act, patches)
        mixed_heads, mixed_far = yield mixed_heads, core_swap(mixed_heads)
        attn_full = yield from whole("attn")
        attn_out = multiply(mixed_heads, attn_full)
        middle = inputs + gate_attn * attn_out
        second_in = modulate(middle, scale_mlp, shift_mlp).astype(jnp.bfloat16)
        middle, second_in, second_in_far = yield middle, second_in, core_swap(second_in)
        up_full = yield from whole("up")
        up_pre = multiply(second_in, up_full)
        up_act = gelu_tanh(up_pre).astype(jnp.bfloat16)
        up_pre, up_act, up_act_far = yield up_pre, up_act, core_swap(up_act)
        down_full = yield from whole("down")
        down_out = multiply(up_act, down_full)
        output_low = (middle + gate_mlp * down_out).astype(jnp.bfloat16)
        down_out, output_low, output_far = yield down_out, output_low, core_swap(output_low)
        first_full = yield from whole("first")
        first_pre = multiply(output_low, first_full)
        first_act = jax.nn.silu(first_pre).astype(jnp.bfloat16)
        first_pre, first_act, first_act_far = yield first_pre, first_act, core_swap(first_act)
        second_full = yield from whole("second")
        second_pre = multiply(first_act, second_full)
        second_act = jax.nn.silu(second_pre).astype(jnp.bfloat16)
        second_pre, second_act, second_far = yield second_pre, second_act, core_swap(second_act)
        third_full = yield from whole("third")
        projected = multiply(second_act, third_full)
        targets = features.reshape(row_count, features.shape[2]).astype(jnp.float32)

        def repa_term(values):
            unit_proj = values * lax.rsqrt(
                jnp.sum(values * values, axis=-1, keepdims=True) + eps_norm
            )
            unit_target = targets * lax.rsqrt(
                jnp.sum(targets * targets, axis=-1, keepdims=True) + eps_norm
            )
            cosine = jnp.sum(unit_proj * unit_target, axis=-1)
            return -lambda_repa * ZDIM * jnp.sum(cosine * valid_rows)

        grad_proj = jax.vjp(repa_term, projected)[1](jnp.float32(1.0))[0].astype(jnp.bfloat16)
        proj_far = core_swap(grad_proj)
        grad_second_pre = silu_back(second_pre, contract_cols(grad_proj, third_full)).astype(
            jnp.bfloat16
        )
        grad_proj, proj_far, grad_second_pre, grad_second_far = (
            yield grad_proj, proj_far, grad_second_pre, core_swap(grad_second_pre)
        )
        give("third", (second_act, second_far), (grad_proj, proj_far))
        give("second", (first_act, first_act_far), (grad_second_pre, grad_second_far))
        grad_first_pre = silu_back(first_pre, contract_cols(grad_second_pre, second_full)).astype(
            jnp.bfloat16
        )
        grad_first_pre, grad_first_far = yield grad_first_pre, core_swap(grad_first_pre)
        give("first", (output_low, output_far), (grad_first_pre, grad_first_far))
        cotangent_rows = (
            cotangent.reshape(row_count, model_width).astype(jnp.float32) * valid_rows[:, None]
        )
        grad_output = contract_cols(grad_first_pre, first_full) + cotangent_rows
        grad_gate_mlp = jnp.sum(grad_output * down_out, axis=0)
        grad_down_in = (gate_mlp * grad_output).astype(jnp.bfloat16)
        grad_output, grad_down_in, grad_down_far = (
            yield grad_output, grad_down_in, core_swap(grad_down_in)
        )
        give("down", (up_act, up_act_far), (grad_down_in, grad_down_far))
        grad_up_pre = gelu_back(up_pre, contract_cols(grad_down_in, down_full)).astype(
            jnp.bfloat16
        )
        grad_up_pre, grad_up_far = yield grad_up_pre, core_swap(grad_up_pre)
        give("up", (second_in, second_in_far), (grad_up_pre, grad_up_far))
        middle_pull = jax.vjp(modulate, middle, scale_mlp, shift_mlp)[1]
        grad_middle_norm, grad_scale_mlp, grad_shift_mlp = middle_pull(
            contract_cols(grad_up_pre, up_full)
        )
        grad_middle = grad_output + grad_middle_norm
        grad_gate_attn = jnp.sum(grad_middle * attn_out, axis=0)
        grad_attn_in = (gate_attn * grad_middle).astype(jnp.bfloat16)
        grad_middle, grad_attn_in, grad_attn_far = (
            yield grad_middle, grad_attn_in, core_swap(grad_attn_in)
        )
        give("attn", (mixed_heads, mixed_far), (grad_attn_in, grad_attn_far))
        grad_mixed = contract_cols(grad_attn_in, attn_full).astype(jnp.bfloat16)
        grad_qkv_in = attention_back(qkv_act, grad_mixed, patches)
        grad_qkv_in, grad_qkv_far = yield grad_qkv_in, core_swap(grad_qkv_in)
        give("qkv", (first_in, first_in_far), (grad_qkv_in, grad_qkv_far))
        input_pull = jax.vjp(modulate, inputs, scale_attn, shift_attn)[1]
        grad_input_norm, grad_scale_attn, grad_shift_attn = input_pull(
            contract_cols(grad_qkv_in, qkv_full)
        )
        grad_input = grad_middle + grad_input_norm
        return (
            output_low,
            grad_input,
            [
                grad_shift_attn,
                grad_scale_attn,
                grad_gate_attn,
                grad_shift_mlp,
                grad_scale_mlp,
                grad_gate_mlp,
            ],
        )

    board.start("compute", compute())
    board.run()
    output_low, grad_input, mod_parts = board.results["compute"]
    grad_modulation = jnp.concatenate(mod_parts)

    def gradient(name):
        parts = [board.results[key] for key in grad_names[name]]
        splits = [Split(*shapes[name], 1, *pair) for pair in back_pairs[name]]
        return whole_gradient(splits, parts, shapes[name][1])

    shares = grad_modulation.reshape(NZ, NX, -1)
    side = lax.dynamic_index_in_dim(shares, 1 - spot.x, 1, False)
    mine = lax.dynamic_index_in_dim(shares, spot.x, 1, False) + x_swap(side)
    mod_share = lax.dynamic_index_in_dim(mine, spot.z, 0, False)
    for offset in (1, 2, 3):
        sent = lax.dynamic_index_in_dim(mine, (spot.z + offset) % NZ, 0, False)
        mod_share = mod_share + z_send(sent, offset)
    core_mods = order_pair(spot.core == 1, mod_share, core_swap(mod_share), 0)
    mods_matrix = order_pair(spot.y == 1, core_mods, y_swap(core_mods), 0).reshape(4, -1)
    act_part = lax.dot_general(
        mods_matrix,
        ada_weight.astype(jnp.float32),
        (((1,), (1,)), ((), ())),
        precision=lax.Precision.HIGHEST,
    )
    grad_condition = silu_back(condition, sum_fsdp(act_part))
    hidden_part = lax.dot_general(
        grad_condition,
        time_second.astype(jnp.float32),
        (((1,), (1,)), ((), ())),
        precision=lax.Precision.HIGHEST,
    )
    grad_hidden = gather_small(hidden_part, spot).transpose(1, 0, 2).reshape(4, -1)
    grad_time_pre = silu_back(time_pre, grad_hidden)

    def outer(left, right):
        return lax.dot_general(
            left, right, (((0,), (0,)), ((), ())), precision=lax.Precision.HIGHEST
        )

    grad_ada = outer(cond_act, mods_matrix)
    grad_bias = jnp.sum(mods_matrix, axis=0)
    sum_tfirst = outer(embedded, grad_time_pre)
    sum_tsecond = outer(hidden_rows, grad_condition)
    grad_cols = take(grad_condition, shard_index * col_count, col_count, 1)
    sum_table = outer(onehot.astype(jnp.float32), grad_cols)
    return (
        output_low.reshape(images, patches, model_width),
        grad_input.reshape(images, patches, model_width),
        gradient("qkv"),
        gradient("attn"),
        gradient("up"),
        gradient("down"),
        gradient("first"),
        gradient("second"),
        gradient("third"),
        grad_ada,
        grad_bias,
        sum_tfirst,
        sum_tsecond,
        sum_table,
    )


def solution(mesh):
    in_specs = (
        P(("bin", "fsdp"), None, None),
        P(("bin", "fsdp"), None, None),
        P(("bin", "fsdp"), None, None),
        P(),
        P(),
        P(),
        P("fsdp", None),
        P("fsdp", None),
        P("fsdp", None),
        P("fsdp", None),
        P("fsdp", None),
        P("fsdp", None),
        P("fsdp", None),
        P(None, "fsdp"),
        P("fsdp"),
        P("fsdp", None),
        P("fsdp", None),
        P(None, "fsdp"),
    )
    out_specs = (
        P(("bin", "fsdp"), None, None),
        P(("bin", "fsdp"), None, None),
        P("fsdp", None),
        P("fsdp", None),
        P("fsdp", None),
        P("fsdp", None),
        P("fsdp", None),
        P("fsdp", None),
        P("fsdp", None),
        P(None, "fsdp"),
        P("fsdp"),
        P("fsdp", None),
        P("fsdp", None),
        P(None, "fsdp"),
    )
    torus = mesh.shape["bin"] == 4 and mesh.shape["fsdp"] == NZ * NX
    step = torus_body if torus else body
    return jax.shard_map(step, mesh=mesh, in_specs=in_specs, out_specs=out_specs, check_vma=False)
```
